32 devices in a mesh: box: 16 (over z, y, x), tile: 2 (over core).
Axes of the slice: x: 2, y: 2, z: 4, core: 2. Of those that a mesh axis runs over, the one named last changes fastest.
Arguments:
- atom_pos: bfloat16 [3, 16384], P(None, ('box', 'tile')), may hold values from 0 to 12
- atom_feat: bfloat16 [16384, 256], P(('box', 'tile')), may hold values from -6 to 6
- tile_cells: int32 [32], P(('box', 'tile')), may hold values from 0 to 1, as said below
- atom_pairs: int32 [128, 6], P(('box', 'tile')), may hold values from 0 to 35, as said below
- atom_counts: int32 [128], P(('box', 'tile')), may hold values from 1 to 6, as said below
- probe_pos: bfloat16 [3, 16384], P(None, ('box', 'tile')), may hold values from 0 to 12
- probe_pairs: int32 [128, 4], P(('box', 'tile')), may hold values from 0 to 35, as said below
- probe_counts: int32 [128], P(('box', 'tile')), may hold values from 1 to 4, as said below
- filt_atom: bfloat16 [20, 256], replicated, may hold values from -1.25 to 1.25
- upd_first: bfloat16 [256, 256], replicated, may hold values from -0.375 to 0.375
- upd_second: bfloat16 [256, 256], replicated, may hold values from -0.375 to 0.375
- filt_probe: bfloat16 [20, 256], replicated, may hold values from -1.25 to 1.25
- read_first: bfloat16 [256, 256], replicated, may hold values from -0.375 to 0.375
- read_out: bfloat16 [256], replicated, may hold values from -0.375 to 0.375
Outputs:
- atom_out: bfloat16 [16384, 256], P(('box', 'tile'))
- density: float32 [16384], P(('box', 'tile'))
The draws below stay inside these ranges and needn't reach their ends.
Inputs may be any that keep to these rules, and one draw needn't show every extreme that they name: `tile_cells`: each run of 2 entries that belongs to one box index holds every z slab number exactly once. `atom_pairs`: each row holds 6 different source block numbers of the atom window. `atom_counts`: at least one entry over all cells equals 6. `probe_pairs`: each row holds 4 different source block numbers of the atom window. `probe_counts`: at least one entry over all cells equals 4.
All inputs are finite; a program needn't handle non-finite values.
Results may differ from the reference program's by a relative error of at most 0.0069.
Values may be sent and summed in bfloat16 or wider, within the bound.
A program may use at most 64 MiB of HBM per device.

```python
import jax
import jax.numpy as jnp
from jax import lax

F = 256
NR = 20
BLOCK = 128
CELL = 12
ATOM_DEV = 512
PROBE_DEV = 512
KMAX = 6
KP = 4
BOXES = 16
TILES = 2
CELLS = 32
ATOMS = 16384
PROBES = 16384
ABLK = 4
PBLK = 4


def draw_tile_cells(key, part):
    keys = jax.random.split(jax.random.fold_in(key, 11), BOXES)

    def one_column(column_key):
        return jax.random.permutation(column_key, TILES)
    return jax.vmap(one_column)(keys).reshape(-1).astype(jnp.int32)


def pick_lists(key, rows_total, list_width, choices_total):
    keys = jax.random.split(key, rows_total)

    def one_row(row_key):
        return jax.random.permutation(row_key, choices_total)[:list_width]
    return jax.vmap(one_row)(keys).astype(jnp.int32)


def ragged_counts(key, blocks_total, most_total):
    first_key, second_key, third_key = jax.random.split(key, 3)
    ceilings = jax.random.randint(first_key, (CELLS, 1), 1, most_total + 1)
    raw_values = jax.random.randint(second_key, (CELLS, blocks_total), 0, 720720)
    counts_drawn = (1 + raw_values % ceilings).reshape(-1)
    full_index = jax.random.randint(third_key, (), 0, CELLS * blocks_total)
    slot_ids = jnp.arange(CELLS * blocks_total, dtype=jnp.int32)
    counts_drawn = jnp.where(slot_ids == full_index, most_total, counts_drawn)
    return counts_drawn.astype(jnp.int32)


def draw_atom_pairs(key, part):
    return pick_lists(jax.random.fold_in(key, 21), CELLS * ABLK, KMAX, 9 * ABLK)


def draw_atom_counts(key, part):
    return ragged_counts(jax.random.fold_in(key, 31), ABLK, KMAX)


def draw_probe_pairs(key, part):
    return pick_lists(jax.random.fold_in(key, 41), CELLS * PBLK, KP, 9 * ABLK)


def draw_probe_counts(key, part):
    return ragged_counts(jax.random.fold_in(key, 51), PBLK, KP)


def levels(key, shape, pieces, least, high):
    def one(position, blocks):
        draws = jax.random.uniform(jax.random.fold_in(jax.random.fold_in(key, 6), position), (blocks,), jnp.float32, least / len(pieces), high / len(pieces))
        return jnp.repeat(jnp.exp(draws), shape[position] // blocks).reshape((-1,) + (1,) * (len(shape) - position - 1))

    level = one(*pieces[0])
    for cut in pieces[1:]:
        level = level * one(*cut)
    return level


def noise(rng, shape, deviation, most, cuts=(), kind=jnp.bfloat16):
    values = jax.random.normal(rng, shape, jnp.float32) * deviation
    if len(cuts) > 0:
        values = levels(rng, shape, cuts, -0.22, 0.18) * values
    return jnp.clip(values, min=-most, max=most).astype(kind)


def setup_inputs(seed: int = 0) -> dict:
    key_list = jax.random.split(jax.random.key(seed), 15)
    return {
        "atom_pos": jnp.clip(12.0 * jax.random.uniform(key_list[0], (3, ATOMS), jnp.float32) ** levels(key_list[0], (3, ATOMS), ((1, 32),), -0.2, 0.2), 0.0, 12.0).astype(jnp.bfloat16),
        "atom_feat": noise(key_list[1], (ATOMS, F), 1.0, 6.0, ((0, 32),)),
        "tile_cells": draw_tile_cells(jax.random.fold_in(key_list[14], 71), 0),
        "atom_pairs": draw_atom_pairs(jax.random.fold_in(key_list[14], 71), 0),
        "atom_counts": draw_atom_counts(jax.random.fold_in(key_list[14], 71), 0),
        "probe_pos": jnp.clip(12.0 * jax.random.uniform(key_list[5], (3, PROBES), jnp.float32) ** levels(key_list[5], (3, PROBES), ((1, 32),), -0.2, 0.2), 0.0, 12.0).astype(jnp.bfloat16),
        "probe_pairs": draw_probe_pairs(jax.random.fold_in(key_list[14], 71), 0),
        "probe_counts": draw_probe_counts(jax.random.fold_in(key_list[14], 71), 0),
        "filt_atom": noise(key_list[8], (NR, F), NR ** -0.5, 1.25),
        "upd_first": noise(key_list[9], (F, F), F ** -0.5, 0.375),
        "upd_second": noise(key_list[10], (F, F), F ** -0.5, 0.375),
        "filt_probe": noise(key_list[11], (NR, F), NR ** -0.5, 1.25),
        "read_first": noise(key_list[12], (F, F), F ** -0.5, 0.375),
        "read_out": noise(key_list[13], (F,), F ** -0.5, 0.375),
    }


cutoff_radius = 5.0

def shifted_softplus(argument):
    return jax.nn.softplus(argument) - jnp.log(2.0)

def basis_block(target_pos, source_pos, keep_mask):
    delta_pos = target_pos[:, :, None] - source_pos[:, None, :]
    distance = jnp.sqrt(lax.optimization_barrier(jnp.sum(delta_pos * delta_pos, axis=0)))
    spacing = cutoff_radius / (NR - 1)
    centers = spacing * jnp.arange(NR, dtype=jnp.float32)
    envelope = jnp.where(distance < cutoff_radius, 0.5 * (jnp.cos(jnp.pi * distance / cutoff_radius) + 1.0), 0.0)
    ratio = (distance[None] - centers[:, None, None]) / spacing
    gaussian = jnp.exp(-0.5 * ratio * ratio)
    return (gaussian * (envelope * keep_mask)[None]).astype(jnp.bfloat16)

def build_window(table_pos, table_feat, box_index, slab_index):
    pos_parts = []
    feat_parts = []
    for shift_x in (-1, 0, 1):
        for shift_z in (-1, 0, 1):
            near_box = ((box_index + shift_x) % BOXES).astype(jnp.int32)
            near_slab = ((slab_index + shift_z) % TILES).astype(jnp.int32)
            pos_here = table_pos[:, near_box, near_slab].astype(jnp.float32)
            offset = jnp.array([shift_x * CELL, 0.0, shift_z * CELL], dtype=jnp.float32)
            pos_parts.append(pos_here + offset[:, None])
            feat_parts.append(table_feat[near_box, near_slab])
    return (jnp.concatenate(pos_parts, axis=1), jnp.concatenate(feat_parts, axis=0))

def collect(target_pos, win_pos, win_feat, pairs, counts, filters, self_check):
    filt_wide = filters.astype(jnp.float32)
    results = []
    for block_index in range(pairs.shape[0]):
        target_here = target_pos[:, block_index * BLOCK:(block_index + 1) * BLOCK]
        running = jnp.zeros((BLOCK, F), jnp.float32)
        for slot_index in range(pairs.shape[1]):
            source = pairs[block_index, slot_index].astype(jnp.int32)
            start = (source * BLOCK).astype(jnp.int32)
            source_pos = lax.dynamic_slice_in_dim(win_pos, start, BLOCK, 1)
            source_feat = lax.dynamic_slice_in_dim(win_feat, start, BLOCK, 0)
            live = (slot_index < counts[block_index]).astype(jnp.float32)
            keep_mask = jnp.ones((BLOCK, BLOCK), jnp.float32)
            if self_check:
                same_block = (source == 4 * ABLK + block_index).astype(jnp.float32)
                keep_mask = keep_mask - same_block * jnp.eye(BLOCK, dtype=jnp.float32)
            keep_mask = keep_mask * live
            basis = basis_block(target_here, source_pos, keep_mask)
            scaled = (source_feat.astype(jnp.float32)[None] * filt_wide[:, None, :]).astype(jnp.bfloat16)
            running = running + jnp.einsum('rij,rjf->if', basis.astype(jnp.float32), scaled.astype(jnp.float32))
        results.append(running)
    return jnp.concatenate(results, axis=0)

def reference(atom_pos, atom_feat, tile_cells, atom_pairs, atom_counts, probe_pos, probe_pairs, probe_counts, filt_atom, upd_first, upd_second, filt_probe, read_first, read_out):
    table_pos = atom_pos.reshape(3, BOXES, TILES, ATOM_DEV)
    table_feat = atom_feat.reshape(BOXES, TILES, ATOM_DEV, F)
    atom_lists = atom_pairs.reshape(CELLS, ABLK, KMAX)
    atom_sizes = atom_counts.reshape(CELLS, ABLK)
    probe_lists = probe_pairs.reshape(CELLS, PBLK, KP)
    probe_sizes = probe_counts.reshape(CELLS, PBLK)
    probe_table = probe_pos.reshape(3, CELLS, PROBE_DEV)

    def update_cell(cell_index):
        box_index = cell_index // TILES
        slab_index = cell_index % TILES
        win_pos, win_feat = build_window(table_pos, table_feat, box_index, slab_index)
        own_pos = win_pos[:, 4 * ATOM_DEV:5 * ATOM_DEV]
        own_feat = win_feat[4 * ATOM_DEV:5 * ATOM_DEV]
        messages = collect(own_pos, win_pos, win_feat, atom_lists[cell_index], atom_sizes[cell_index], filt_atom, True)
        hidden = shifted_softplus(jnp.dot(messages.astype(jnp.bfloat16), upd_first, preferred_element_type=jnp.float32)).astype(jnp.bfloat16)
        change = jnp.dot(hidden, upd_second, preferred_element_type=jnp.float32)
        return (own_feat.astype(jnp.float32) + change).astype(jnp.bfloat16)
    updated = lax.map(update_cell, jnp.arange(CELLS, dtype=jnp.int32))
    fresh_table = updated.reshape(BOXES, TILES, ATOM_DEV, F)

    def readout_cell(cell_index):
        box_index = cell_index // TILES
        slab_index = tile_cells[cell_index].astype(jnp.int32)
        win_pos, win_feat = build_window(table_pos, fresh_table, box_index, slab_index)
        points_here = probe_table[:, cell_index].astype(jnp.float32)
        features = collect(points_here, win_pos, win_feat, probe_lists[cell_index], probe_sizes[cell_index], filt_probe, False)
        hidden = shifted_softplus(jnp.dot(features.astype(jnp.bfloat16), read_first, preferred_element_type=jnp.float32)).astype(jnp.bfloat16)
        return jnp.dot(hidden, read_out, preferred_element_type=jnp.float32)
    density = lax.map(readout_cell, jnp.arange(CELLS, dtype=jnp.int32)).reshape(PROBES)
    return (updated.reshape(ATOMS, F), density)
```

```python
import functools
import math

import jax
import jax.numpy as jnp
from jax import lax
from jax.experimental import pallas as pl
from jax.experimental.pallas import tpu as pltpu
from jax.sharding import PartitionSpec as P

BLOCK = 128
CELL = 12.0
CUTOFF = 5.0
VMEM_LIMIT = 48 * 1024 * 1024


def shifted_softplus(v):
    return jnp.maximum(v, 0.0) + jnp.log1p(jnp.exp(-jnp.abs(v))) - math.log(2.0)


def halo(mine, count):
    tail = lax.ppermute(mine, "box", [(i, (i + 1) % count) for i in range(count)])
    head = lax.ppermute(mine, "box", [((i + 1) % count, i) for i in range(count)])
    return jnp.concatenate([tail, mine, head], axis=0)


def spread_filter(filt_ref, wide_ref):
    count = filt_ref.shape[0]
    mid = count // 2
    filt = filt_ref[...].astype(jnp.float32)
    for r in range(count):
        row = filt[r : r + 1, :] * math.exp(-0.5 * (r - mid) ** 2)
        wide_ref[r] = jnp.broadcast_to(row, wide_ref.shape[1:]).astype(jnp.bfloat16)


def basis_terms(tx, ty, tz, sx, sy, sz, count, self_flag):
    dx, dy, dz = tx - sx, ty - sy, tz - sz
    square = dx * dx + dy * dy + dz * dz
    inside = square < CUTOFF * CUTOFF
    if self_flag is not None:
        rows = lax.broadcasted_iota(jnp.int32, square.shape, 0)
        cols = lax.broadcasted_iota(jnp.int32, square.shape, 1)
        inside = jnp.logical_and(inside, rows - cols != self_flag)
    square = jnp.minimum(square, CUTOFF * CUTOFF)
    angle = square * (math.pi / (2.0 * CUTOFF)) ** 2
    cosine = jnp.full_like(angle, 1.0 / math.factorial(12))
    for n in (10, 8, 6, 4, 2, 0):
        cosine = cosine * angle + (-1.0) ** (n // 2) / math.factorial(n)
    mid = count // 2
    ratio = jnp.sqrt(square) * ((count - 1) / CUTOFF) - mid
    middle = jnp.where(inside, cosine * cosine * jnp.exp(-0.5 * ratio * ratio), 0.0)
    up, down = jnp.exp(ratio), jnp.exp(-ratio)
    terms = [None] * count
    terms[mid] = middle
    for r in range(mid + 1, count):
        terms[r] = terms[r - 1] * up
    for r in range(mid - 1, -1, -1):
        terms[r] = terms[r + 1] * down
    return [t.astype(jnp.bfloat16) for t in terms]


def gather_messages(block, slab, tiles, pairs, counts, target, pos, feat, wide, acc, self_check):
    nb = pairs.shape[0]
    cols = [
        jnp.broadcast_to(target[block, n : n + 1, :], (BLOCK, BLOCK)).T for n in range(3)
    ]
    acc[...] = jnp.zeros_like(acc)

    def slot(k, carry):
        q = pairs[block, k]
        cell = q // nb
        step_x, step_z = cell // 3, lax.rem(cell, 3)
        near = lax.rem(slab + step_z + (tiles - 1), tiles)
        where = (step_x * tiles + near) * nb + lax.rem(q, nb)
        shift_x = (step_x - 1).astype(jnp.float32) * CELL
        shift_z = (step_z - 1).astype(jnp.float32) * CELL
        flag = None
        if self_check:
            flag = jnp.where(q == 4 * nb + block, 0, 2 * BLOCK)
        spot = pos[where]
        terms = basis_terms(
            *cols,
            spot[0:1, :] + shift_x,
            spot[1:2, :],
            spot[2:3, :] + shift_z,
            wide.shape[0],
            flag,
        )
        source = feat[where].reshape(BLOCK // 16, 16, feat.shape[-1])
        scaled = [
            (source * wide[r][None]).reshape(BLOCK, feat.shape[-1]) for r in range(wide.shape[0])
        ]
        acc[...] += jnp.dot(
            jnp.concatenate(terms, axis=1),
            jnp.concatenate(scaled, axis=0),
            preferred_element_type=jnp.float32,
        )
        return carry

    lax.fori_loop(0, counts[block], slot, 0)


def atom_kernel(
    tiles, pairs, counts, slab, target, pos, feat, filt, first, second, own, out, wide, acc
):
    spread_filter(filt, wide)
    def each(block, carry):
        gather_messages(
            block, slab[0], tiles, pairs, counts, target, pos, feat, wide, acc, True
        )
        hidden = shifted_softplus(
            jnp.dot(
                acc[...].astype(jnp.bfloat16), first[...], preferred_element_type=jnp.float32
            )
        ).astype(jnp.bfloat16)
        change = jnp.dot(hidden, second[...], preferred_element_type=jnp.float32)
        out[block] = (own[block].astype(jnp.float32) + change).astype(jnp.bfloat16)
        return carry

    lax.fori_loop(0, pairs.shape[0], each, 0)


def probe_kernel(
    tiles, pairs, counts, slab, target, pos, feat, filt, first, last, out, wide, acc
):
    spread_filter(filt, wide)
    def each(block, carry):
        gather_messages(
            block, slab[0], tiles, pairs, counts, target, pos, feat, wide, acc, False
        )
        hidden = shifted_softplus(
            jnp.dot(
                acc[...].astype(jnp.bfloat16), first[...], preferred_element_type=jnp.float32
            )
        ).astype(jnp.bfloat16)
        lifted = hidden.astype(jnp.float32) * last[...].astype(jnp.float32)
        out[block] = jnp.sum(lifted.T, axis=0, keepdims=True)
        return carry

    lax.fori_loop(0, pairs.shape[0], each, 0)


def shards(
    tiles,
    boxes,
    atom_pos,
    atom_feat,
    tile_cells,
    atom_pairs,
    atom_counts,
    probe_pos,
    probe_pairs,
    probe_counts,
    filt_atom,
    upd_first,
    upd_second,
    filt_probe,
    read_first,
    read_out,
):
    atoms, width = atom_feat.shape
    nb = atoms // BLOCK
    count = filt_atom.shape[0]

    def blocks_of(pos):
        return pos.reshape(3, -1, BLOCK).transpose(1, 0, 2).astype(jnp.float32)

    def columns(mine):
        column = lax.all_gather(mine, "tile", axis=0, tiled=True)
        return halo(column, boxes)

    smem = pl.BlockSpec(memory_space=pltpu.SMEM)
    vmem = pl.BlockSpec(memory_space=pltpu.VMEM)
    scratch = [
        pltpu.VMEM((count, 16, width), jnp.bfloat16),
        pltpu.VMEM((BLOCK, width), jnp.float32),
    ]
    params = pltpu.CompilerParams(vmem_limit_bytes=VMEM_LIMIT)
    own_pos = blocks_of(atom_pos)
    own_feat = atom_feat.reshape(nb, BLOCK, width)
    pos = columns(own_pos)
    here = lax.axis_index("tile").astype(jnp.int32).reshape(1)
    fresh = pl.pallas_call(
        functools.partial(atom_kernel, tiles),
        out_shape=jax.ShapeDtypeStruct((nb, BLOCK, width), jnp.bfloat16),
        in_specs=[smem] * 3 + [vmem] * 7,
        out_specs=vmem,
        scratch_shapes=scratch,
        compiler_params=params,
    )(
        atom_pairs,
        atom_counts,
        here,
        own_pos,
        pos,
        columns(own_feat),
        filt_atom,
        upd_first,
        upd_second,
        own_feat,
    )
    probe_blocks = blocks_of(probe_pos)
    density = pl.pallas_call(
        functools.partial(probe_kernel, tiles),
        out_shape=jax.ShapeDtypeStruct((probe_blocks.shape[0], 1, BLOCK), jnp.float32),
        in_specs=[smem] * 3 + [vmem] * 6,
        out_specs=vmem,
        scratch_shapes=scratch,
        compiler_params=params,
    )(
        probe_pairs,
        probe_counts,
        tile_cells,
        probe_blocks,
        pos,
        columns(fresh),
        filt_probe,
        read_first,
        read_out.reshape(1, width),
    )
    return (fresh.reshape(atoms, width), density.reshape(-1))


def solution(mesh):
    both = ("box", "tile")
    placed = (
        P(None, both),
        P(both, None),
        P(both),
        P(both, None),
        P(both),
        P(None, both),
        P(both, None),
        P(both),
    ) + (P(),) * 6
    return jax.shard_map(
        functools.partial(shards, mesh.shape["tile"], mesh.shape["box"]),
        mesh=mesh,
        in_specs=placed,
        out_specs=(P(both, None), P(both)),
        check_vma=False,
    )
```

```python
import functools
import math

import jax
import jax.numpy as jnp
from jax import lax
from jax.experimental import pallas as pl
from jax.experimental.pallas import tpu as pltpu
from jax.sharding import PartitionSpec as P

BLOCK = 128
CELL = 12.0
CUTOFF = 5.0
VMEM_LIMIT = 56 * 1024 * 1024
MESH = pl.DeviceIdType.MESH


def shifted_softplus(v):
    return jnp.maximum(v, 0.0) + jnp.log1p(jnp.exp(-jnp.abs(v))) - math.log(2.0)


def spread_filter(filt_ref, wide_ref):
    count = filt_ref.shape[0]
    mid = count // 2
    filt = filt_ref[...].astype(jnp.float32)
    for r in range(count):
        row = filt[r : r + 1, :] * math.exp(-0.5 * (r - mid) ** 2)
        wide_ref[r] = jnp.broadcast_to(row, wide_ref.shape[1:]).astype(jnp.bfloat16)


def basis_terms(tx, ty, tz, sx, sy, sz, count, limit, self_flag):
    dx, dy, dz = tx - sx, ty - sy, tz - sz
    square = dx * dx + dy * dy + dz * dz
    inside = square < limit
    if self_flag is not None:
        rows = lax.broadcasted_iota(jnp.int32, square.shape, 0)
        cols = lax.broadcasted_iota(jnp.int32, square.shape, 1)
        inside = jnp.logical_and(inside, rows - cols != self_flag)
    square = jnp.minimum(square, CUTOFF * CUTOFF)
    angle = square * (math.pi / (2.0 * CUTOFF)) ** 2
    cosine = jnp.full_like(angle, 1.0 / math.factorial(12))
    for n in (10, 8, 6, 4, 2, 0):
        cosine = cosine * angle + (-1.0) ** (n // 2) / math.factorial(n)
    mid = count // 2
    ratio = jnp.sqrt(square) * ((count - 1) / CUTOFF) - mid
    middle = jnp.where(inside, cosine * cosine * jnp.exp(-0.5 * ratio * ratio), 0.0)
    up, down = jnp.exp(ratio), jnp.exp(-ratio)
    terms = [None] * count
    terms[mid] = middle
    for r in range(mid + 1, count):
        terms[r] = terms[r - 1] * up
    for r in range(mid - 1, -1, -1):
        terms[r] = terms[r + 1] * down
    return [t.astype(jnp.bfloat16) for t in terms]


class Flow:
    def __init__(self, place, table, cell_rows, chunk_rows, sems):
        self.place, self.table, self.sems = place, table, sems
        self.cell_rows, self.chunk_rows = cell_rows, chunk_rows

    def rows(self, column, chunk):
        _, tile, _, tiles = self.place
        start = (column * tiles + tile) * self.cell_rows + chunk * self.chunk_rows
        return self.table.at[pl.ds(start, self.chunk_rows)]

    def copy(self, source, column, chunk, kind, box, tile):
        return pltpu.make_async_remote_copy(
            src_ref=source,
            dst_ref=self.rows(column, chunk),
            send_sem=self.sems.at[0, kind, chunk],
            recv_sem=self.sems.at[1, kind, chunk],
            device_id=(box, tile),
            device_id_type=MESH,
        )

    def copies(self, chunk, source=None):
        box, tile, boxes, tiles = self.place
        odd = lax.rem(box, 2)
        partner = box + 1 - 2 * odd
        onward = lax.rem(box + 2 - 4 * odd + boxes, boxes)
        from_partner, from_far = 2 - 2 * odd, 2 * odd
        source = self.rows(1, chunk) if source is None else source
        stages = [
            [self.copy(source, from_far, chunk, 0, partner, tile)],
            [self.copy(self.rows(from_partner, chunk), from_far, chunk, 1, onward, tile)],
            [],
        ]
        columns = [1, from_partner, from_far]
        for n in range(1, tiles):
            other = lax.rem(tile + n, tiles)
            for stage in range(3):
                origin = source if stage == 0 else self.rows(columns[stage], chunk)
                kind = 2 + stage * (tiles - 1) + n - 1
                stages[stage].append(
                    self.copy(origin, columns[stage], chunk, kind, box, other)
                )
        return stages

    def begin(self, chunk, source=None):
        for copy in self.copies(chunk, source)[0]:
            copy.start()

    def pass_partner(self, chunk, source=None):
        stages = self.copies(chunk, source)
        stages[0][0].wait_recv()
        for copy in stages[1]:
            copy.start()

    def pass_far(self, chunk, source=None):
        stages = self.copies(chunk, source)
        stages[1][0].wait_recv()
        for copy in stages[2]:
            copy.start()

    def finish(self, chunk, source=None):
        stages = self.copies(chunk, source)
        for copy in stages[0][1:] + stages[1][1:] + stages[2]:
            copy.wait_recv()

    def drain(self, chunk, source=None):
        for stage in self.copies(chunk, source):
            for copy in stage:
                copy.wait_send()


def greet(place):
    box, tile, boxes, tiles = place
    odd = lax.rem(box, 2)
    barrier = pltpu.get_barrier_semaphore()
    for near in (box + 1 - 2 * odd, lax.rem(box + 2, boxes), lax.rem(box + boxes - 2, boxes)):
        pl.semaphore_signal(barrier, inc=1, device_id=(near, tile), device_id_type=MESH)
    for n in range(1, tiles):
        pl.semaphore_signal(
            barrier, inc=1, device_id=(box, lax.rem(tile + n, tiles)), device_id_type=MESH
        )
    return lambda: pl.semaphore_wait(barrier, 3 + tiles - 1)


def kernel(
    boxes,
    tiles,
    atom_pairs,
    atom_counts,
    probe_pairs,
    probe_counts,
    probe_slab,
    own_pos,
    probe_pos,
    own,
    filt_atom,
    first,
    second,
    filt_probe,
    read_first,
    read_out,
    out,
    density,
    pos,
    feat,
    fresh,
    columns,
    atom_basis,
    probe_basis,
    wide_atom,
    wide_probe,
    pos_sems,
    feat_sems,
    fresh_sems,
):
    box, tile = lax.axis_index("box"), lax.axis_index("tile")
    place = (box, tile, boxes, tiles)
    blocks, most = atom_pairs.shape
    points, least = probe_pairs.shape
    count, _, width = wide_atom.shape
    ready = greet(place)

    own_rows = (tiles + tile) * blocks
    spread_filter(filt_atom, wide_atom)
    spread_filter(filt_probe, wide_probe)
    for part, targets in ((0, own_pos), (blocks, probe_pos)):

        def lay(block, carry, part=part, targets=targets):
            rows = targets[block]
            for n in range(3):
                columns[part + block, n] = jnp.broadcast_to(rows[n : n + 1], (BLOCK, BLOCK)).T
            return carry

        lax.fori_loop(0, targets.shape[0], lay, 0)
    pos[pl.ds(own_rows, blocks)] = own_pos[...]
    feat[pl.ds(own_rows, blocks)] = own[...]

    def locate(q, slab):
        cell = q // blocks
        step_x, step_z = cell // 3, lax.rem(cell, 3)
        near = lax.rem(slab + step_z + (tiles - 1), tiles)
        where = (step_x * tiles + near) * blocks + lax.rem(q, blocks)
        return where, step_x, step_z

    def basis(pair, pairs, counts, slab, part, store, self_check):
        block, k = pair // pairs.shape[1], lax.rem(pair, pairs.shape[1])
        q = pairs[block, k]
        where, step_x, step_z = locate(q, slab)
        shift_x = (step_x - 1).astype(jnp.float32) * CELL
        shift_z = (step_z - 1).astype(jnp.float32) * CELL
        limit = jnp.where(k < counts[block], CUTOFF * CUTOFF, -1.0)
        flag = jnp.where(q == 4 * blocks + block, 0, 2 * BLOCK) if self_check else None
        spot = pos[where]
        terms = basis_terms(
            columns[part + block, 0],
            columns[part + block, 1],
            columns[part + block, 2],
            spot[0:1, :] + shift_x,
            spot[1:2, :],
            spot[2:3, :] + shift_z,
            count,
            limit,
            flag,
        )
        for r in range(count):
            store[pair, :, r * BLOCK : (r + 1) * BLOCK] = terms[r]

    def messages(block, pairs, slab, table, wide, store):
        total = None
        for k in range(pairs.shape[1]):
            where, _, _ = locate(pairs[block, k], slab)
            source = table[where].reshape(BLOCK // 16, 16, width)
            scaled = [(source * wide[r][None]).reshape(BLOCK, width) for r in range(count)]
            part = jnp.dot(
                store[block * pairs.shape[1] + k],
                jnp.concatenate(scaled, axis=0),
                preferred_element_type=jnp.float32,
            )
            total = part if total is None else total + part
        return total.astype(jnp.bfloat16)

    def loop(start, stop, body):
        def step(n, carry):
            body(n)
            return carry

        lax.fori_loop(start, stop, step, 0)

    def atom_basis_of(pair):
        basis(pair, atom_pairs, atom_counts, tile, 0, atom_basis, True)

    def probe_basis_of(pair):
        basis(pair, probe_pairs, probe_counts, probe_slab[0], blocks, probe_basis, False)

    pos_flow = Flow(place, pos, blocks, blocks, pos_sems)
    feat_flow = Flow(place, feat, blocks, 1, feat_sems)
    fresh_flow = Flow(place, fresh, blocks, 1, fresh_sems)

    ready()
    pos_flow.begin(0)
    loop(0, blocks, feat_flow.begin)
    pos_flow.pass_partner(0)
    pos_flow.pass_far(0)
    pos_flow.finish(0)

    share = most // 2

    def pass_on_partner(chunk):
        feat_flow.pass_partner(chunk)
        loop(chunk * share, (chunk + 1) * share, atom_basis_of)

    def pass_on_far(chunk):
        feat_flow.pass_far(chunk)
        loop((blocks + chunk) * share, (blocks + chunk + 1) * share, atom_basis_of)

    loop(0, blocks, pass_on_partner)
    loop(0, blocks, pass_on_far)
    loop(2 * blocks * share, blocks * most, atom_basis_of)
    loop(0, blocks, feat_flow.finish)

    def update(block):
        total = messages(block, atom_pairs, tile, feat, wide_atom, atom_basis)
        hidden = shifted_softplus(
            jnp.dot(total, first[...], preferred_element_type=jnp.float32)
        ).astype(jnp.bfloat16)
        change = jnp.dot(hidden, second[...], preferred_element_type=jnp.float32)
        changed = (own[block].astype(jnp.float32) + change).astype(jnp.bfloat16)
        out[block] = changed
        fresh[own_rows + block] = changed
        fresh_flow.begin(block)

        @pl.when(block > 0)
        def _():
            fresh_flow.pass_partner(block - 1)

    loop(0, blocks, update)
    fresh_flow.pass_partner(blocks - 1)
    each = (points * least) // blocks

    def pass_on_fresh(chunk):
        fresh_flow.pass_far(chunk)
        loop(chunk * each, (chunk + 1) * each, probe_basis_of)

    loop(0, blocks, pass_on_fresh)
    loop(blocks * each, points * least, probe_basis_of)
    loop(0, blocks, fresh_flow.finish)

    def read(block):
        total = messages(block, probe_pairs, probe_slab[0], fresh, wide_probe, probe_basis)
        hidden = shifted_softplus(
            jnp.dot(total, read_first[...], preferred_element_type=jnp.float32)
        ).astype(jnp.bfloat16)
        lifted = hidden.astype(jnp.float32) * read_out[...].astype(jnp.float32)
        density[block] = jnp.sum(lifted.T, axis=0, keepdims=True)

    loop(0, points, read)
    pos_flow.drain(0)
    loop(0, blocks, feat_flow.drain)
    loop(0, blocks, fresh_flow.drain)


def shards(
    tiles,
    boxes,
    atom_pos,
    atom_feat,
    tile_cells,
    atom_pairs,
    atom_counts,
    probe_pos,
    probe_pairs,
    probe_counts,
    filt_atom,
    upd_first,
    upd_second,
    filt_probe,
    read_first,
    read_out,
):
    atoms, width = atom_feat.shape
    nb = atoms // BLOCK
    count = filt_atom.shape[0]
    points = probe_pairs.shape[0]
    rows = 3 * tiles * nb
    kinds = 2 + 3 * (tiles - 1)

    def blocks_of(pos):
        laid = pos.reshape(3, -1, BLOCK).transpose(1, 0, 2).astype(jnp.float32)
        return jnp.pad(laid, ((0, 0), (0, 5), (0, 0)))

    smem = pl.BlockSpec(memory_space=pltpu.SMEM)
    vmem = pl.BlockSpec(memory_space=pltpu.VMEM)
    fresh, density = pl.pallas_call(
        functools.partial(kernel, boxes, tiles),
        out_shape=(
            jax.ShapeDtypeStruct((nb, BLOCK, width), jnp.bfloat16),
            jax.ShapeDtypeStruct((points, 1, BLOCK), jnp.float32),
        ),
        in_specs=[smem] * 5 + [vmem] * 9,
        out_specs=(vmem, vmem),
        scratch_shapes=[
            pltpu.VMEM((rows, 8, BLOCK), jnp.float32),
            pltpu.VMEM((rows, BLOCK, width), jnp.bfloat16),
            pltpu.VMEM((rows, BLOCK, width), jnp.bfloat16),
            pltpu.VMEM((nb + points, 3, BLOCK, BLOCK), jnp.float32),
            pltpu.VMEM((nb * atom_pairs.shape[1], BLOCK, count * BLOCK), jnp.bfloat16),
            pltpu.VMEM((points * probe_pairs.shape[1], BLOCK, count * BLOCK), jnp.bfloat16),
            pltpu.VMEM((count, 16, width), jnp.bfloat16),
            pltpu.VMEM((count, 16, width), jnp.bfloat16),
            pltpu.SemaphoreType.DMA((2, kinds, 1)),
            pltpu.SemaphoreType.DMA((2, kinds, nb)),
            pltpu.SemaphoreType.DMA((2, kinds, nb)),
        ],
        compiler_params=pltpu.CompilerParams(
            collective_id=0, has_side_effects=True, vmem_limit_bytes=VMEM_LIMIT
        ),
    )(
        atom_pairs,
        atom_counts,
        probe_pairs,
        probe_counts,
        tile_cells,
        blocks_of(atom_pos),
        blocks_of(probe_pos),
        atom_feat.reshape(nb, BLOCK, width),
        filt_atom,
        upd_first,
        upd_second,
        filt_probe,
        read_first,
        read_out.reshape(1, width),
    )
    return (fresh.reshape(atoms, width), density.reshape(-1))


def solution(mesh):
    both = ("box", "tile")
    placed = (
        P(None, both),
        P(both, None),
        P(both),
        P(both, None),
        P(both),
        P(None, both),
        P(both, None),
        P(both),
    ) + (P(),) * 6
    return jax.shard_map(
        functools.partial(shards, mesh.shape["tile"], mesh.shape["box"]),
        mesh=mesh,
        in_specs=placed,
        out_specs=(P(both, None), P(both)),
        check_vma=False,
    )
```

```python
import functools
import math

import jax
import jax.numpy as jnp
from jax import lax
from jax.experimental import pallas as pl
from jax.experimental.pallas import tpu as pltpu
from jax.sharding import PartitionSpec as P

BLOCK = 128
CELL = 12.0
CUTOFF = 5.0
VMEM_LIMIT = 56 * 1024 * 1024
MESH = pl.DeviceIdType.MESH


def shifted_softplus(v):
    return jnp.maximum(v, 0.0) + jnp.log(1.0 + jnp.exp(-jnp.abs(v))) - math.log(2.0)


def spread_filter(filt_ref, wide_ref):
    count = filt_ref.shape[0]
    mid = count // 2
    filt = filt_ref[...].astype(jnp.float32)
    for r in range(count):
        row = filt[r : r + 1, :] * math.exp(-0.5 * (r - mid) ** 2)
        wide_ref[r] = jnp.broadcast_to(row, wide_ref.shape[1:]).astype(jnp.bfloat16)


def basis_terms(tx, ty, tz, sx, sy, sz, count, limit, self_flag):
    dx, dy, dz = tx - sx, ty - sy, tz - sz
    square = dx * dx + dy * dy + dz * dz
    inside = square < limit
    if self_flag is not None:
        rows = lax.broadcasted_iota(jnp.int32, square.shape, 0)
        cols = lax.broadcasted_iota(jnp.int32, square.shape, 1)
        inside = jnp.logical_and(inside, rows - cols != self_flag)
    square = jnp.minimum(square, CUTOFF * CUTOFF)
    angle = square * (math.pi / (2.0 * CUTOFF)) ** 2
    cosine = jnp.full_like(angle, 1.0 / math.factorial(12))
    for n in (10, 8, 6, 4, 2, 0):
        cosine = cosine * angle + (-1.0) ** (n // 2) / math.factorial(n)
    mid = count // 2
    ratio = jnp.sqrt(square) * ((count - 1) / CUTOFF) - mid
    middle = jnp.where(inside, cosine * cosine * jnp.exp(-0.5 * ratio * ratio), 0.0)
    up, down = jnp.exp(ratio), jnp.exp(-ratio)
    terms = [None] * count
    terms[mid] = middle
    for r in range(mid + 1, count):
        terms[r] = terms[r - 1] * up
    for r in range(mid - 1, -1, -1):
        terms[r] = terms[r + 1] * down
    return [t.astype(jnp.bfloat16) for t in terms]


class Flow:
    def __init__(self, place, table, cell_rows, chunk_rows, sems):
        self.place, self.table, self.sems = place, table, sems
        self.cell_rows, self.chunk_rows = cell_rows, chunk_rows

    def rows(self, column, chunk):
        _, tile, _, tiles = self.place
        start = (column * tiles + tile) * self.cell_rows + chunk * self.chunk_rows
        return self.table.at[pl.ds(start, self.chunk_rows)]

    def copy(self, source, column, chunk, kind, box, tile):
        return pltpu.make_async_remote_copy(
            src_ref=source,
            dst_ref=self.rows(column, chunk),
            send_sem=self.sems.at[0, kind, chunk],
            recv_sem=self.sems.at[1, kind, chunk],
            device_id=(box, tile),
            device_id_type=MESH,
        )

    def copies(self, chunk, source=None):
        box, tile, boxes, tiles = self.place
        odd = lax.rem(box, 2)
        partner = box + 1 - 2 * odd
        onward = lax.rem(box + 2 - 4 * odd + boxes, boxes)
        from_partner, from_far = 2 - 2 * odd, 2 * odd
        source = self.rows(1, chunk) if source is None else source
        stages = [
            [self.copy(source, from_far, chunk, 0, partner, tile)],
            [self.copy(self.rows(from_partner, chunk), from_far, chunk, 1, onward, tile)],
            [],
        ]
        columns = [1, from_partner, from_far]
        for n in range(1, tiles):
            other = lax.rem(tile + n, tiles)
            for stage in range(3):
                origin = source if stage == 0 else self.rows(columns[stage], chunk)
                kind = 2 + stage * (tiles - 1) + n - 1
                stages[stage].append(
                    self.copy(origin, columns[stage], chunk, kind, box, other)
                )
        return stages

    def begin(self, chunk, source=None):
        for copy in self.copies(chunk, source)[0]:
            copy.start()

    def pass_partner(self, chunk, source=None):
        stages = self.copies(chunk, source)
        stages[0][0].wait_recv()
        for copy in stages[1]:
            copy.start()

    def pass_far(self, chunk, source=None):
        stages = self.copies(chunk, source)
        stages[1][0].wait_recv()
        for copy in stages[2]:
            copy.start()

    def finish(self, chunk, source=None):
        stages = self.copies(chunk, source)
        for copy in stages[0][1:] + stages[1][1:] + stages[2]:
            copy.wait_recv()

    def drain(self, chunk, source=None):
        for stage in self.copies(chunk, source):
            for copy in stage:
                copy.wait_send()


def greet(place):
    box, tile, boxes, tiles = place
    barrier = pltpu.get_barrier_semaphore()
    met = [(lax.rem(box + 2, boxes), tile), (lax.rem(box + boxes - 2, boxes), tile)]
    met += [near for _, _, near in around(place)]
    for near in met:
        pl.semaphore_signal(barrier, inc=1, device_id=near, device_id_type=MESH)
    return lambda: pl.semaphore_wait(barrier, len(met))


def around(place):
    box, tile, boxes, tiles = place
    return [
        (step, n, (lax.rem(box + step + boxes, boxes), lax.rem(tile + n, tiles)))
        for step in (-1, 1, 0)
        for n in range(tiles)
        if step != 0 or n > 0
    ]


def send_positions(place, table, rows, sems):
    _, tile, _, tiles = place
    copies = []
    for step, n, near in around(place):
        kind = (step + 1) * tiles + n
        copies.append(
            pltpu.make_async_remote_copy(
                src_ref=table.at[pl.ds((tiles + tile) * rows, rows)],
                dst_ref=table.at[pl.ds(((1 - step) * tiles + tile) * rows, rows)],
                send_sem=sems.at[0, kind],
                recv_sem=sems.at[1, kind],
                device_id=near,
                device_id_type=MESH,
            )
        )
        copies[-1].start()
    return copies


def kernel(
    boxes,
    tiles,
    atom_pairs,
    atom_counts,
    probe_pairs,
    probe_counts,
    probe_slab,
    own_pos,
    probe_pos,
    own,
    filt_atom,
    first,
    second,
    filt_probe,
    read_first,
    read_out,
    out,
    density,
    pos,
    feat,
    fresh,
    columns,
    atom_basis,
    probe_basis,
    wide_atom,
    wide_probe,
    pos_sems,
    feat_sems,
    fresh_sems,
):
    box, tile = lax.axis_index("box"), lax.axis_index("tile")
    place = (box, tile, boxes, tiles)
    blocks, most = atom_pairs.shape
    points, least = probe_pairs.shape
    count, _, width = wide_atom.shape
    ready = greet(place)

    own_rows = (tiles + tile) * blocks
    def prepare():
        spread_filter(filt_atom, wide_atom)
        spread_filter(filt_probe, wide_probe)
        for part, targets in ((0, own_pos), (blocks, probe_pos)):
            for n in range(3):
                row = targets[n : n + 1, :].astype(jnp.float32)
                for block in range(targets.shape[1] // BLOCK):
                    cut = row[:, block * BLOCK : (block + 1) * BLOCK]
                    columns[part + block, n] = jnp.broadcast_to(cut, (BLOCK, BLOCK)).T

    mine = own_pos[...].astype(jnp.float32)
    for block in range(blocks):
        pos[own_rows + block, 0:3, :] = mine[:, block * BLOCK : (block + 1) * BLOCK]
        pos[own_rows + block, 3:8, :] = jnp.zeros((5, BLOCK), jnp.float32)
    feat[pl.ds(own_rows, blocks)] = own[...]

    def locate(q, slab):
        cell = q // blocks
        step_x, step_z = cell // 3, lax.rem(cell, 3)
        near = lax.rem(slab + step_z + (tiles - 1), tiles)
        where = (step_x * tiles + near) * blocks + lax.rem(q, blocks)
        return where, step_x, step_z

    def basis(pair, pairs, counts, slab, part, store, self_check):
        block, k = pair // pairs.shape[1], lax.rem(pair, pairs.shape[1])
        q = pairs[block, k]
        where, step_x, step_z = locate(q, slab)
        shift_x = (step_x - 1).astype(jnp.float32) * CELL
        shift_z = (step_z - 1).astype(jnp.float32) * CELL
        limit = jnp.where(k < counts[block], CUTOFF * CUTOFF, -1.0)
        flag = jnp.where(q == 4 * blocks + block, 0, 2 * BLOCK) if self_check else None
        spot = pos[where]
        terms = basis_terms(
            columns[part + block, 0],
            columns[part + block, 1],
            columns[part + block, 2],
            spot[0:1, :] + shift_x,
            spot[1:2, :],
            spot[2:3, :] + shift_z,
            count,
            limit,
            flag,
        )
        for r in range(count):
            store[pair, :, r * BLOCK : (r + 1) * BLOCK] = terms[r]

    def messages(block, pairs, slab, table, wide, store):
        total = None
        for k in range(pairs.shape[1]):
            where, _, _ = locate(pairs[block, k], slab)
            source = table[where].reshape(BLOCK // 16, 16, width)
            scaled = [(source * wide[r][None]).reshape(BLOCK, width) for r in range(count)]
            part = jnp.dot(
                store[block * pairs.shape[1] + k],
                jnp.concatenate(scaled, axis=0),
                preferred_element_type=jnp.float32,
            )
            total = part if total is None else total + part
        return total.astype(jnp.bfloat16)

    def loop(start, stop, body):
        def step(n, carry):
            body(n)
            return carry

        lax.fori_loop(start, stop, step, 0)

    def atom_basis_of(pair):
        basis(pair, atom_pairs, atom_counts, tile, 0, atom_basis, True)

    def probe_basis_of(pair):
        basis(pair, probe_pairs, probe_counts, probe_slab[0], blocks, probe_basis, False)

    feat_flow = Flow(place, feat, blocks, 1, feat_sems)
    fresh_flow = Flow(place, fresh, blocks, 1, fresh_sems)

    prepare()
    ready()
    sent = send_positions(place, pos, blocks, pos_sems)
    loop(0, blocks, feat_flow.begin)
    for copy in sent:
        copy.wait_recv()

    steps = blocks + 2
    share = blocks * most // steps

    def pass_on(n):
        @pl.when(n < blocks)
        def _():
            feat_flow.pass_partner(n)

        @pl.when(n >= 2)
        def _():
            feat_flow.pass_far(n - 2)

        loop(n * share, (n + 1) * share, atom_basis_of)

    loop(0, steps, pass_on)
    if steps * share < blocks * most:
        loop(steps * share, blocks * most, atom_basis_of)
    loop(0, blocks, feat_flow.finish)

    def update(block):
        total = messages(block, atom_pairs, tile, feat, wide_atom, atom_basis)
        hidden = shifted_softplus(
            jnp.dot(total, first[...], preferred_element_type=jnp.float32)
        ).astype(jnp.bfloat16)
        change = jnp.dot(hidden, second[...], preferred_element_type=jnp.float32)
        changed = (own[block].astype(jnp.float32) + change).astype(jnp.bfloat16)
        out[block] = changed
        fresh[own_rows + block] = changed
        fresh_flow.begin(block)

        @pl.when(block >= 2)
        def _():
            fresh_flow.pass_partner(block - 2)

    loop(0, blocks, update)
    each = points * least // blocks

    def pass_on_fresh(n):
        @pl.when(n < 2)
        def _():
            fresh_flow.pass_partner(blocks - 2 + n)

        fresh_flow.pass_far(n)
        loop(n * each, (n + 1) * each, probe_basis_of)

    loop(0, blocks, pass_on_fresh)
    if blocks * each < points * least:
        loop(blocks * each, points * least, probe_basis_of)
    loop(0, blocks, fresh_flow.finish)

    def read(block):
        total = messages(block, probe_pairs, probe_slab[0], fresh, wide_probe, probe_basis)
        hidden = shifted_softplus(
            jnp.dot(total, read_first[...], preferred_element_type=jnp.float32)
        ).astype(jnp.bfloat16)
        last = jnp.broadcast_to(read_out[...].reshape(1, width), (16, width))
        summed = lax.dot_general(
            last, hidden, (((1,), (1,)), ((), ())), preferred_element_type=jnp.float32
        )
        density[block] = summed[0:1, :]

    loop(0, points, read)
    for copy in sent:
        copy.wait_send()
    loop(0, blocks, feat_flow.drain)
    loop(0, blocks, fresh_flow.drain)


def shards(
    tiles,
    boxes,
    atom_pos,
    atom_feat,
    tile_cells,
    atom_pairs,
    atom_counts,
    probe_pos,
    probe_pairs,
    probe_counts,
    filt_atom,
    upd_first,
    upd_second,
    filt_probe,
    read_first,
    read_out,
):
    atoms, width = atom_feat.shape
    nb = atoms // BLOCK
    count = filt_atom.shape[0]
    points = probe_pairs.shape[0]
    rows = 3 * tiles * nb
    kinds = 2 + 3 * (tiles - 1)

    smem = pl.BlockSpec(memory_space=pltpu.SMEM)
    vmem = pl.BlockSpec(memory_space=pltpu.VMEM)
    fresh, density = pl.pallas_call(
        functools.partial(kernel, boxes, tiles),
        out_shape=(
            jax.ShapeDtypeStruct((nb, BLOCK, width), jnp.bfloat16),
            jax.ShapeDtypeStruct((points, 1, BLOCK), jnp.float32),
        ),
        in_specs=[smem] * 5 + [vmem] * 9,
        out_specs=(vmem, vmem),
        scratch_shapes=[
            pltpu.VMEM((rows, 8, BLOCK), jnp.float32),
            pltpu.VMEM((rows, BLOCK, width), jnp.bfloat16),
            pltpu.VMEM((rows, BLOCK, width), jnp.bfloat16),
            pltpu.VMEM((nb + points, 3, BLOCK, BLOCK), jnp.float32),
            pltpu.VMEM((nb * atom_pairs.shape[1], BLOCK, count * BLOCK), jnp.bfloat16),
            pltpu.VMEM((points * probe_pairs.shape[1], BLOCK, count * BLOCK), jnp.bfloat16),
            pltpu.VMEM((count, 16, width), jnp.bfloat16),
            pltpu.VMEM((count, 16, width), jnp.bfloat16),
            pltpu.SemaphoreType.DMA((2, 3 * tiles)),
            pltpu.SemaphoreType.DMA((2, kinds, nb)),
            pltpu.SemaphoreType.DMA((2, kinds, nb)),
        ],
        compiler_params=pltpu.CompilerParams(
            collective_id=0, has_side_effects=True, vmem_limit_bytes=VMEM_LIMIT
        ),
    )(
        atom_pairs,
        atom_counts,
        probe_pairs,
        probe_counts,
        tile_cells,
        atom_pos,
        probe_pos,
        atom_feat.reshape(nb, BLOCK, width),
        filt_atom,
        upd_first,
        upd_second,
        filt_probe,
        read_first,
        read_out.reshape(1, width),
    )
    return (fresh.reshape(atoms, width), density.reshape(-1))


def solution(mesh):
    both = ("box", "tile")
    placed = (
        P(None, both),
        P(both, None),
        P(both),
        P(both, None),
        P(both),
        P(None, both),
        P(both, None),
        P(both),
    ) + (P(),) * 6
    return jax.shard_map(
        functools.partial(shards, mesh.shape["tile"], mesh.shape["box"]),
        mesh=mesh,
        in_specs=placed,
        out_specs=(P(both, None), P(both)),
        check_vma=False,
    )
```
